32 devices in a mesh: dp: 2 (over y), expert: 16 (over z, x, core).
Axes of the slice: x: 2, y: 2, z: 4, core: 2. Of those that a mesh axis runs over, the one named last changes fastest.
Arguments:
- grad_out: bfloat16 [8192, 4096], P('expert', 'dp'), may hold values from -30 to 30
- hidden: bfloat16 [8192, 2, 1024], P('expert', None, 'dp'), may hold values from -24 to 24
- gate_prob: float32 [8192, 2], P('expert'), may hold values from 0.05 to 1
- expert_ids: int32 [8192, 2], P('expert'), may hold values from 0 to 15, all different within a row; in each aligned block of 512 rows (0 to 511, 512 to 1023, ...) at most 80 rows name the same one
- weights: bfloat16 [16, 1024, 4096], P('expert', None, 'dp'), may hold values from -0.1875 to 0.1875
Outputs:
- hidden_grad: bfloat16 [8192, 2, 1024], P('expert', None, 'dp')
- update: float32 [16, 1024, 4096], P('expert', None, 'dp')
The draws below stay inside these ranges and needn't reach their ends.
Inputs may be any that keep to these rules, and one draw needn't show every extreme that they name: `expert_ids`: among the 512 tokens of one index of expert, no expert is named by more than 80 choices, a bound that some block reaches; the 2 experts of a token differ.
All inputs are finite; a program needn't handle non-finite values.
Results may differ from the reference program's by a relative error of at most 0.019.
Values may be sent and summed in bfloat16 or wider, within the bound.
A program may use at most 64 MiB of HBM per device.

```python
import math
import jax
import jax.numpy as jnp
import numpy as np
from jax import lax

D = 4096
F = 1024
TOPK = 2
TOK_DEV = 512
NEXP = 16
CAP = 80
TOKENS = 8192
N_DP = 2
N_EXPERT = 16


def draw_grad_out(key, part):
    key_noise = jax.random.fold_in(key, 11)
    key_scale = jax.random.fold_in(key, 12)
    column = jnp.arange(D, dtype=jnp.float32) / D
    spread = jnp.exp(jnp.log(3.0) * column + jnp.log(3.4) * jax.random.uniform(key_scale, (D,), jnp.float32))
    noise_part = jax.random.normal(key_noise, (TOKENS, D), jnp.float32)
    values = noise_part
    return jnp.clip(0.4 * values * spread[None, :], -30.0, 30.0).astype(jnp.bfloat16)


def draw_hidden(key, part):
    key_noise = jax.random.fold_in(key, 21)
    key_scale = jax.random.fold_in(key, 22)
    unit_scale = jnp.exp(jnp.log(10.0) * jax.random.uniform(key_scale, (F,), jnp.float32))
    noise_part = jax.random.normal(key_noise, (TOKENS, TOPK, F), jnp.float32)
    return jnp.clip(0.3 * noise_part * unit_scale, -24.0, 24.0).astype(jnp.bfloat16)


def steps_of(rng, dims, split, least, top_value):
    loudness, own = 1.0, jax.random.fold_in(rng, 6)
    for position, shards_of in split:
        steps = jnp.exp(jax.random.uniform(jax.random.fold_in(own, position), (shards_of,), jnp.float32, least / len(split), top_value / len(split)))
        loudness = loudness * jnp.repeat(steps, dims[position] // shards_of).reshape([-1 if axis == position else 1 for axis in range(len(dims))])
    return loudness


def routed_block(own_key, own, number, rows, count, top, most, skew):
    sequence = jax.random.permutation(own_key, count)
    crowded, common = portions_of(count, rows * top, most, skew, True), portions_of(count, rows * top, most, skew, False)
    places = jnp.arange(count)

    def named(lengths, rotation):
        used = int((lengths > 0).sum())
        fixed = max(1, used // 4)
        moved = fixed + (places - fixed + rotation * (used - fixed)) % max(1, count - fixed)
        return jnp.zeros((count,), jnp.int32).at[sequence[jnp.where(places < fixed, places, moved)]].set(jnp.asarray(lengths, jnp.int32))

    lengths = jnp.where(number % 4 == 0, named(crowded, number // 4), named(common, number - number // 4 - 1))
    mixed = jax.random.permutation(jax.random.fold_in(own, 3), count)
    donor, receiver = mixed[0:count // 2 * 2:2], mixed[1:count // 2 * 2:2]
    margin = jnp.minimum(lengths[donor] - 1, most - lengths[receiver]) // 2
    margin = jnp.where((donor == sequence[0]) | (receiver == sequence[0]) | (lengths[receiver] == 0), 0, jnp.maximum(margin, 0))
    moved = jax.random.randint(jax.random.fold_in(own, 4), (count // 2,), 0, 1 << 20) % (margin + 1)
    lengths = lengths.at[donor].add(-moved).at[receiver].add(moved)
    items = jnp.searchsorted(jnp.cumsum(lengths), jnp.arange(rows * top), side="right").astype(jnp.int32)
    listing = items.reshape(top, rows).T
    listing = listing[jax.random.permutation(jax.random.fold_in(own, 1), rows)]
    rotation = jax.random.randint(jax.random.fold_in(own, 2), (rows, 1), 0, top)
    return jnp.take_along_axis(listing, (jnp.arange(top)[None, :] + rotation) % top, axis=1)


def portions_of(count, total, bound, skew, full):
    loads = [(1 << 20) // math.isqrt(rank ** skew) + 1 for rank in range(1, count + 1)]
    largest = bound if full else min(bound, max(-(-total // count), total * loads[0] // sum(loads)))
    least = 1 if total - largest >= count - 1 else 0
    holding, surplus = [largest] + [least] * (count - 1), total - largest - least * (count - 1)
    while surplus > 0:
        free = [i for i in range(1, count) if holding[i] < largest] or [i for i in range(1, count) if holding[i] < bound]
        pool, left = sum([loads[i] for i in free]), surplus
        for i in free:
            addition = min(bound - holding[i], max(1, left * loads[i] // pool), surplus)
            holding[i] = holding[i] + addition
            surplus = surplus - addition
    return np.array(holding)


def noise(own_key, shape, scale, reach, split=(), held_as=jnp.bfloat16):
    loudness = steps_of(own_key, shape, split, -0.22, 0.18) if split else 1.0
    array = jax.random.normal(own_key, shape, jnp.float32) * scale * loudness
    return jnp.minimum(jnp.maximum(array, -reach), reach).astype(held_as)


def setup_inputs(seed: int = 0) -> dict:
    key_list = jax.random.split(jax.random.key(seed), 6)
    grad_out = draw_grad_out(jax.random.fold_in(key_list[5], 71), 0)
    hidden = draw_hidden(jax.random.fold_in(key_list[5], 71), 0)
    gate_prob = jnp.clip(0.05 + 0.95 * jax.random.uniform(key_list[2], (TOKENS, TOPK), jnp.float32) ** steps_of(key_list[2], (TOKENS, TOPK), ((0, 16),), -0.2, 0.2), 0.05, 1.0)
    expert_ids_keys = jax.random.split(jax.random.fold_in(key_list[3], 1), TOKENS // TOK_DEV)
    expert_ids_turns = jax.random.permutation(jax.random.fold_in(key_list[3], 3), TOKENS // TOK_DEV)
    expert_ids = jax.vmap(lambda own, number: routed_block(jax.random.fold_in(key_list[3], 2), own, number, TOK_DEV, NEXP, TOPK, CAP, 1))(expert_ids_keys, expert_ids_turns).reshape((TOKENS, TOPK))
    weights = noise(key_list[4], (NEXP, F, D), F ** -0.5, 0.1875, ((0, 16), (2, 2)))
    return {"grad_out": grad_out, "hidden": hidden, "gate_prob": gate_prob, "expert_ids": expert_ids, "weights": weights}


def slot_numbers(route_ids, capacity, expert_count):
    flat_ids = route_ids.reshape(-1)
    one_hot = (flat_ids[:, None] == jnp.arange(expert_count, dtype=jnp.int32)[None, :]).astype(jnp.int32)
    before = jnp.cumsum(one_hot, axis=0) - one_hot
    rank_in = lax.optimization_barrier(jnp.sum(before * one_hot, axis=1))
    return (flat_ids * capacity + rank_in).astype(jnp.int32)

def rounded(value):
    return lax.optimization_barrier(value.astype(jnp.bfloat16)).astype(jnp.float32)

def block_gram(matrix_b):
    width_part = D // N_DP
    gram_total = jnp.zeros((F, F), jnp.float32)
    for block_number in range(N_DP):
        column_piece = matrix_b[:, block_number * width_part:(block_number + 1) * width_part]
        gram_total = gram_total + rounded(jnp.dot(column_piece, column_piece.T, preferred_element_type=jnp.float32))
    return gram_total

def reference(grad_out, hidden, gate_prob, expert_ids, weights):
    pair_count = TOK_DEV * TOPK
    total_slots = NEXP * CAP
    width_part = D // N_DP
    source_ids = expert_ids.reshape(N_EXPERT, TOK_DEV, TOPK)
    slot_index = jax.vmap(lambda route_part: slot_numbers(route_part, CAP, NEXP))(source_ids)
    source_rows = jnp.arange(N_EXPERT, dtype=jnp.int32)[:, None]
    owner_table = jnp.full((N_EXPERT, total_slots), pair_count, jnp.int32)
    owner_table = owner_table.at[source_rows, slot_index].set(jnp.arange(pair_count, dtype=jnp.int32)[None, :])
    flat_hidden = hidden.reshape(N_EXPERT * pair_count, F)
    flat_prob = gate_prob.reshape(-1)

    def one_expert(packed):
        expert_number, weight_matrix = packed
        chosen = lax.dynamic_slice_in_dim(owner_table, (expert_number * CAP).astype(jnp.int32), CAP, 1)
        is_valid = chosen < pair_count
        safe_pair = jnp.where(is_valid, chosen, 0)
        global_pair = (source_rows * pair_count + safe_pair).reshape(-1).astype(jnp.int32)
        is_valid = is_valid.reshape(-1)
        token_rows = global_pair // TOPK
        grad_rows = jnp.where(is_valid[:, None], grad_out[token_rows], 0)
        prob_rows = jnp.where(is_valid, flat_prob[global_pair], 0.0)
        scaled = (prob_rows[:, None] * flat_hidden[global_pair].astype(jnp.float32)).astype(jnp.bfloat16)
        gradient = jnp.dot(scaled.T, grad_rows, preferred_element_type=jnp.float32)
        grad_bf16 = gradient.astype(jnp.bfloat16)
        back_total = jnp.zeros((total_slots, F), jnp.float32)
        for block_number in range(N_DP):
            column_start = block_number * width_part
            column_end = column_start + width_part
            block_term = jnp.dot(grad_rows[:, column_start:column_end], weight_matrix[:, column_start:column_end].T, preferred_element_type=jnp.float32)
            back_total = back_total + rounded(block_term)
        gram_first = block_gram(grad_bf16)
        norm_sq = jnp.sqrt(jnp.sum(gram_first * gram_first)) + 1e-06
        current = (grad_bf16.astype(jnp.float32) * lax.rsqrt(norm_sq)).astype(jnp.bfloat16)
        gram_now = (gram_first / norm_sq).astype(jnp.bfloat16)
        following = current.astype(jnp.float32)
        for sweep_number in range(2):
            if sweep_number > 0:
                gram_now = block_gram(current).astype(jnp.bfloat16)
            following = 1.5 * current.astype(jnp.float32) - 0.5 * jnp.dot(gram_now, current, preferred_element_type=jnp.float32)
            current = following.astype(jnp.bfloat16)
        return (back_total, following * D ** 0.5)
    slot_grads, update = lax.map(one_expert, (jnp.arange(NEXP, dtype=jnp.int32), weights))
    expert_flat = expert_ids.reshape(N_EXPERT, pair_count)
    slot_row = expert_flat * total_slots + source_rows * CAP + slot_index - expert_flat * CAP
    picked = slot_grads.reshape(NEXP * total_slots, F)[slot_row.reshape(-1).astype(jnp.int32)]
    hidden_grad = (flat_prob[:, None] * picked).astype(jnp.bfloat16).reshape(TOKENS, TOPK, F)
    return (hidden_grad, update)
```

```python
import functools

import jax
import jax.numpy as jnp
from jax import lax
from jax.experimental import pallas as pl
from jax.experimental.pallas import tpu as pltpu
from jax.sharding import PartitionSpec as P

D = 4096
MESH = pl.DeviceIdType.MESH
BF16 = jnp.bfloat16
F32 = jnp.float32
GROUPS = 4


def dot(a, b, dims=((1,), (0,))):
    return lax.dot_general(a, b, (dims, ((), ())), preferred_element_type=F32)


def kernel(
    n, ndp, cap,
    ids_ref, grad_ref, scaled_ref, weight_ref,
    g_ref, p_ref, c_ref, picked_ref,
    rank0, rank1, select, send_grad, got_grad, send_scaled, got_scaled, scaled_t,
    back_part, back_got, summed, returned,
    gram_part, gram_got, gram_sum, a_ref, a2_ref, w_ref,
    grad_s, grad_r, sc_s, sc_r, ret_s, ret_r, ysc_s, ysc_r, yb_s, yb_r, gram_s, gram_r,
):
    d, e = lax.axis_index("dp"), lax.axis_index("expert")
    tokens, width = grad_ref.shape
    rows = n * cap
    part = scaled_ref.shape[1]
    hid = part * ndp
    tile = min(256, part)
    tiles, per_part = hid // tile, part // tile
    own = n // 2
    members = n // GROUPS
    group_rows = members * cap
    chunk = min(512, width)

    def block(j):
        return pl.ds(pl.multiple_of(j * cap, 16), cap)

    def ahead(j):
        return lax.rem(e + lax.rem(j + n // 2, n), n)

    def behind(j):
        return lax.rem(e + n - lax.rem(j + n // 2, n), n)

    def loop(lo, hi, body):
        def step(i, carry):
            body(i)
            return carry
        lax.fori_loop(lo, hi, step, 0)

    def others(body):
        loop(0, own, body)
        loop(own + 1, n, body)

    def dp_peer(p):
        return lax.rem(d + p, ndp)

    barrier = pltpu.get_barrier_semaphore()

    def greet(j):
        pl.semaphore_signal(barrier, inc=1, device_id=(d, ahead(j)), device_id_type=MESH)

    others(greet)
    for p in range(1, ndp):
        pl.semaphore_signal(barrier, inc=1, device_id=(dp_peer(p), e), device_id_type=MESH)

    expert_row = lax.broadcasted_iota(jnp.int32, (n, tokens), 0)
    is0 = ids_ref[0:1, :] == expert_row
    is1 = ids_ref[1:2, :] == expert_row
    named = (jnp.where(is0, 1.0, 0.0) + jnp.where(is1, 1.0, 0.0)).astype(BF16)
    earlier = lax.broadcasted_iota(jnp.int32, (tokens, tokens), 0) < lax.broadcasted_iota(
        jnp.int32, (tokens, tokens), 1
    )
    rank = dot(named, jnp.where(earlier, 1.0, 0.0).astype(BF16))
    rank0[...] = jnp.where(is0, rank, -1.0)
    rank1[...] = jnp.where(is1, rank, -1.0)

    def build(j):
        to = ahead(j)
        slot = lax.broadcasted_iota(jnp.int32, (cap, tokens), 0).astype(F32)
        for k, ref in ((0, rank0), (1, rank1)):
            select[block(j), k * tokens:(k + 1) * tokens] = jnp.where(
                ref[pl.ds(to, 1), :] == slot, 1.0, 0.0
            ).astype(BF16)

    loop(0, n, build)
    pl.semaphore_wait(barrier, n - 1 + ndp - 1)

    def scaled_copy(j, peer):
        return pltpu.make_async_remote_copy(
            src_ref=send_scaled.at[block(j)], dst_ref=got_scaled.at[d, block(j)],
            send_sem=sc_s.at[j], recv_sem=sc_r.at[j], device_id=(d, peer), device_id_type=MESH)

    def grad_copy(j, peer):
        return pltpu.make_async_remote_copy(
            src_ref=send_grad.at[block(j)], dst_ref=got_grad.at[block(j)],
            send_sem=grad_s.at[j], recv_sem=grad_r.at[j], device_id=(d, peer), device_id_type=MESH)

    def return_copy(j, peer):
        return pltpu.make_async_remote_copy(
            src_ref=summed.at[block(j)], dst_ref=returned.at[block(j)],
            send_sem=ret_s.at[j], recv_sem=ret_r.at[j], device_id=(d, peer), device_id_type=MESH)

    def across_scaled(g, p):
        at = pl.ds(g * group_rows, group_rows)
        return pltpu.make_async_remote_copy(
            src_ref=got_scaled.at[d, at], dst_ref=got_scaled.at[d, at],
            send_sem=ysc_s.at[p, g], recv_sem=ysc_r.at[p, g],
            device_id=(dp_peer(p), e), device_id_type=MESH)

    def arrived_scaled(g, p):
        at = pl.ds(g * group_rows, group_rows)
        source = lax.rem(d + ndp - p, ndp)
        return pltpu.make_async_remote_copy(
            src_ref=got_scaled.at[source, at], dst_ref=got_scaled.at[source, at],
            send_sem=ysc_s.at[p, g], recv_sem=ysc_r.at[p, g],
            device_id=(dp_peer(p), e), device_id_type=MESH)

    def across_back(g, p):
        at = pl.ds(g * group_rows, group_rows)
        return pltpu.make_async_remote_copy(
            src_ref=back_part.at[dp_peer(p), at], dst_ref=back_got.at[p - 1, at],
            send_sem=yb_s.at[p, g], recv_sem=yb_r.at[p, g],
            device_id=(dp_peer(p), e), device_id_type=MESH)

    def across_gram(i, p):
        at = (pl.ds(i * tile, tile), pl.ds(0, (i + 1) * tile))
        return pltpu.make_async_remote_copy(
            src_ref=gram_part.at[at], dst_ref=gram_got.at[(p - 1,) + at],
            send_sem=gram_s.at[p, i], recv_sem=gram_r.at[p, i],
            device_id=(dp_peer(p), e), device_id_type=MESH)

    def scaled_rows(j):
        return dot(select[block(j), :], scaled_ref[...]).astype(BF16)

    def grad_rows(j):
        chosen = select[block(j), 0:tokens] + select[block(j), tokens:2 * tokens]
        return dot(chosen, grad_ref[...]).astype(BF16)

    def put_scaled(j):
        send_scaled[block(j), :] = scaled_rows(j)
        scaled_copy(j, ahead(j)).start()

    def put_grad(j):
        send_grad[block(j), :] = grad_rows(j)
        grad_copy(j, ahead(j)).start()

    others(put_scaled)
    others(put_grad)
    got_scaled[d, own * cap:(own + 1) * cap, :] = scaled_rows(own)
    got_grad[own * cap:(own + 1) * cap, :] = grad_rows(own)

    def members_of(g, body):
        first = g * members
        loop(first + (1 if first == own else 0), first + members, body)

    for g in range(GROUPS):
        members_of(g, lambda j: scaled_copy(j, ahead(j)).wait_recv())
        for p in range(1, ndp):
            across_scaled(g, p).start()

    def back_of(g):
        at = slice(g * group_rows, (g + 1) * group_rows)
        members_of(g, lambda j: grad_copy(j, ahead(j)).wait_recv())

        def column(i):
            term = dot(got_grad[at, :], weight_ref[pl.ds(pl.multiple_of(i * tile, tile), tile), :],
                       ((1,), (1,))).astype(BF16)
            cols = pl.ds(pl.multiple_of(lax.rem(i, per_part) * tile, tile), tile)
            back_part[lax.div(i, per_part), at, cols] = term

        loop(0, tiles, column)
        for p in range(1, ndp):
            across_back(g, p).start()

    for g in range(GROUPS):
        if g == GROUPS - 1:
            for h in range(GROUPS):
                for p in range(1, ndp):
                    arrived_scaled(h, p).wait_recv()
            for b in range(ndp):
                scaled_t[b * part:(b + 1) * part, :] = got_scaled[b].T
        back_of(g)

    for i in range(tiles):
        at = slice(i * tile, (i + 1) * tile)

        def gradient(c):
            cols = pl.ds(pl.multiple_of(c * chunk, chunk), chunk)
            g_ref[at, cols] = dot(scaled_t[at, :], got_grad[:, cols]).astype(BF16)

        def gram(j):
            other = pl.ds(pl.multiple_of(j * tile, tile), tile)
            gram_part[at, other] = dot(g_ref[at, :], g_ref[other, :], ((1,), (1,))).astype(BF16)

        loop(0, width // chunk, gradient)
        loop(0, i + 1, gram)
        for p in range(1, ndp):
            across_gram(i, p).start()

    for g in range(GROUPS):
        at = slice(g * group_rows, (g + 1) * group_rows)
        for p in range(1, ndp):
            across_back(g, p).wait_recv()
        total = back_part[d, at, :].astype(F32)
        for p in range(1, ndp):
            total = total + back_got[p - 1, at, :].astype(F32)
        summed[at, :] = total.astype(BF16)
        members_of(g, lambda j: return_copy(j, behind(j)).start())
    returned[own * cap:(own + 1) * cap, :] = summed[own * cap:(own + 1) * cap, :]

    squares = jnp.zeros((1, 1), F32)
    for i in range(tiles):
        at = slice(i * tile, (i + 1) * tile)
        for p in range(1, ndp):
            across_gram(i, p).wait_recv()
        for j in range(i + 1):
            other = slice(j * tile, (j + 1) * tile)
            total = gram_part[at, other].astype(F32)
            for p in range(1, ndp):
                total = total + gram_got[p - 1, at, other].astype(F32)
            gram_sum[at, other] = total
            here = jnp.sum(jnp.sum(total * total, axis=0, keepdims=True), axis=1, keepdims=True)
            squares = squares + here * (1.0 if i == j else 2.0)
    norm_sq = jnp.sqrt(squares) + 1e-6
    inverse = 1.0 / norm_sq
    scale = lax.rsqrt(norm_sq) * (D**0.5)
    c_ref[...] = jnp.broadcast_to(2.25 * scale, c_ref.shape)
    for i in range(tiles):
        at = slice(i * tile, (i + 1) * tile)
        for j in range(i + 1):
            other = slice(j * tile, (j + 1) * tile)
            value = gram_sum[at, other] * inverse
            a_ref[at, other] = value.astype(BF16)
            if j < i:
                a_ref[other, at] = value.T.astype(BF16)

    def square(i):
        at = pl.ds(pl.multiple_of(i * tile, tile), tile)
        a2 = dot(a_ref[at, :], a_ref[...])
        a1 = a_ref[at, :].astype(F32)
        a2_ref[at, :] = a2.astype(BF16)
        w_ref[at, :] = (1.125 * a1 - 0.125 * a2).astype(BF16)
        gram_sum[at, :] = 1.6875 * a2 - 2.4375 * a1

    def finish(i):
        at = pl.ds(pl.multiple_of(i * tile, tile), tile)
        last = dot(a2_ref[at, :], w_ref[...])
        p_ref[at, :] = ((gram_sum[at, :] - 0.5 * last) * scale).astype(BF16)

    loop(0, tiles, square)
    loop(0, tiles, finish)

    others(lambda j: return_copy(j, behind(j)).wait_recv())
    step = min(256, tokens)

    def pick(t):
        cols = pl.ds(pl.multiple_of(t * step, step), step)
        picked_ref[cols, :] = dot(select[:, cols], returned[...], ((0,), (0,))).astype(BF16)

    loop(0, 2 * tokens // step, pick)

    def drain(j):
        scaled_copy(j, ahead(j)).wait_send()
        grad_copy(j, ahead(j)).wait_send()
        return_copy(j, behind(j)).wait_send()

    others(drain)
    for p in range(1, ndp):
        for g in range(GROUPS):
            across_scaled(g, p).wait_send()
            across_back(g, p).wait_send()
        for i in range(tiles):
            across_gram(i, p).wait_send()


def per_device(n, ndp, grad_out, hidden, gate_prob, expert_ids, weights):
    tokens, width = grad_out.shape
    top = expert_ids.shape[1]
    part = hidden.shape[2]
    hid = part * ndp
    capacity = 5 * tokens * top // (4 * n)
    cap = -(-capacity // 16) * 16
    rows = n * cap
    tiles = hid // min(256, part)
    scaled = (gate_prob[:, :, None] * hidden.astype(F32)).astype(BF16)
    scaled = scaled.transpose(1, 0, 2).reshape(top * tokens, part)
    vmem = pl.BlockSpec(memory_space=pltpu.VMEM)
    dma = pltpu.SemaphoreType.DMA
    grads, poly, scale, picked = pl.pallas_call(
        functools.partial(kernel, n, ndp, cap),
        out_shape=[
            jax.ShapeDtypeStruct((hid, width), BF16),
            jax.ShapeDtypeStruct((hid, hid), BF16),
            jax.ShapeDtypeStruct((8, 128), F32),
            jax.ShapeDtypeStruct((top * tokens, part), BF16),
        ],
        in_specs=[vmem] * 4,
        out_specs=[vmem] * 4,
        scratch_shapes=[
            pltpu.VMEM((n, tokens), F32),
            pltpu.VMEM((n, tokens), F32),
            pltpu.VMEM((rows, top * tokens), BF16),
            pltpu.VMEM((rows, width), BF16),
            pltpu.VMEM((rows, width), BF16),
            pltpu.VMEM((rows, part), BF16),
            pltpu.VMEM((ndp, rows, part), BF16),
            pltpu.VMEM((hid, rows), BF16),
            pltpu.VMEM((ndp, rows, part), BF16),
            pltpu.VMEM((ndp - 1, rows, part), BF16),
            pltpu.VMEM((rows, part), BF16),
            pltpu.VMEM((rows, part), BF16),
            pltpu.VMEM((hid, hid), BF16),
            pltpu.VMEM((ndp - 1, hid, hid), BF16),
            pltpu.VMEM((hid, hid), F32),
            pltpu.VMEM((hid, hid), BF16),
            pltpu.VMEM((hid, hid), BF16),
            pltpu.VMEM((hid, hid), BF16),
        ] + [dma((n,))] * 6 + [dma((ndp, GROUPS))] * 4 + [dma((ndp, tiles))] * 2,
        compiler_params=pltpu.CompilerParams(
            collective_id=0, has_side_effects=True, vmem_limit_bytes=62 * 1024 * 1024
        ),
        cost_estimate=pl.CostEstimate(flops=20_000_000_000, bytes_accessed=16_000_000, transcendentals=0),
    )(expert_ids.T, grad_out, scaled, weights[0])
    update = dot(poly, grads) + grads.astype(F32) * scale[0, 0]
    back = picked.reshape(top, tokens, part).transpose(1, 0, 2).astype(F32)
    hidden_grad = (gate_prob[:, :, None] * back).astype(BF16)
    return (hidden_grad, update[None])


def solution(mesh):
    in_specs = (
        P("expert", "dp"),
        P("expert", None, "dp"),
        P("expert", None),
        P("expert", None),
        P("expert", None, "dp"),
    )
    out_specs = (P("expert", None, "dp"), P("expert", None, "dp"))
    return jax.shard_map(
        functools.partial(per_device, mesh.shape["expert"], mesh.shape["dp"]),
        mesh=mesh, in_specs=in_specs, out_specs=out_specs, check_vma=False,
    )
```

```python
import functools

import jax
import jax.numpy as jnp
from jax import lax
from jax.experimental import pallas as pl
from jax.experimental.pallas import tpu as pltpu
from jax.sharding import PartitionSpec as P

D = 4096
MESH = pl.DeviceIdType.MESH
BF16 = jnp.bfloat16
F32 = jnp.float32
GROUPS = 4


def dot(a, b, dims=((1,), (0,))):
    return lax.dot_general(a, b, (dims, ((), ())), preferred_element_type=F32)


def kernel(
    n, ndp, cap,
    ids_ref, prob_ref, grad_ref, scaled_ref, weight_ref,
    g_ref, p_ref, c_ref, picked_ref,
    rank0, rank1, select, send_grad, got_grad, send_scaled, got_scaled, early_t, late_t,
    back_part, back_got, summed, returned,
    gram_part, gram_got, v_part, v_got, gram_sum, a_ref,
    grad_s, grad_r, sc_s, sc_r, ret_s, ret_r, ysc_s, ysc_r, yb_s, yb_r, gram_s, gram_r, v_s, v_r,
):
    d, e = lax.axis_index("dp"), lax.axis_index("expert")
    tokens, width = grad_ref.shape
    rows = n * cap
    part = scaled_ref.shape[1]
    hid = part * ndp
    tile = min(256, part)
    tiles, per_part = hid // tile, part // tile
    own = 0
    members = n // GROUPS
    group_rows = members * cap
    chunk = min(512, width)
    split = rows - group_rows

    def block(j):
        return pl.ds(pl.multiple_of(j * cap, 16), cap)

    def offset(j):
        return lax.rem(j, members) * GROUPS + lax.div(j, members)

    def ahead(j):
        return lax.rem(e + offset(j), n)

    def behind(j):
        return lax.rem(e + n - offset(j), n)

    def loop(lo, hi, body):
        def step(i, carry):
            body(i)
            return carry
        lax.fori_loop(lo, hi, step, 0)

    def others(body):
        loop(1, n, body)

    def dp_peer(p):
        return lax.rem(d + p, ndp)

    barrier = pltpu.get_barrier_semaphore()

    def greet(j):
        pl.semaphore_signal(barrier, inc=1, device_id=(d, ahead(j)), device_id_type=MESH)

    others(greet)
    for p in range(1, ndp):
        pl.semaphore_signal(barrier, inc=1, device_id=(dp_peer(p), e), device_id_type=MESH)

    expert_row = lax.broadcasted_iota(jnp.int32, (n, tokens), 0)
    is0 = ids_ref[0:1, :] == expert_row
    is1 = ids_ref[1:2, :] == expert_row
    named = (jnp.where(is0, 1.0, 0.0) + jnp.where(is1, 1.0, 0.0)).astype(BF16)
    earlier = lax.broadcasted_iota(jnp.int32, (tokens, tokens), 0) < lax.broadcasted_iota(
        jnp.int32, (tokens, tokens), 1
    )
    rank = dot(named, jnp.where(earlier, 1.0, 0.0).astype(BF16))
    rank0[...] = jnp.where(is0, rank, -1.0)
    rank1[...] = jnp.where(is1, rank, -1.0)

    def build(j):
        to = ahead(j)
        slot = lax.broadcasted_iota(jnp.int32, (cap, tokens), 0).astype(F32)
        for k, ref in ((0, rank0), (1, rank1)):
            select[block(j), k * tokens:(k + 1) * tokens] = jnp.where(
                ref[pl.ds(to, 1), :] == slot, 1.0, 0.0
            ).astype(BF16)

    loop(0, n, build)
    pl.semaphore_wait(barrier, n - 1 + ndp - 1)

    def scaled_copy(j, peer):
        return pltpu.make_async_remote_copy(
            src_ref=send_scaled.at[block(j)], dst_ref=got_scaled.at[d, block(j)],
            send_sem=sc_s.at[j], recv_sem=sc_r.at[j], device_id=(d, peer), device_id_type=MESH)

    def grad_copy(j, peer):
        return pltpu.make_async_remote_copy(
            src_ref=send_grad.at[block(j)], dst_ref=got_grad.at[block(j)],
            send_sem=grad_s.at[j], recv_sem=grad_r.at[j], device_id=(d, peer), device_id_type=MESH)

    def return_copy(j, peer):
        return pltpu.make_async_remote_copy(
            src_ref=summed.at[block(j)], dst_ref=returned.at[block(j)],
            send_sem=ret_s.at[j], recv_sem=ret_r.at[j], device_id=(d, peer), device_id_type=MESH)

    def across_scaled(g, p):
        at = pl.ds(g * group_rows, group_rows)
        return pltpu.make_async_remote_copy(
            src_ref=got_scaled.at[d, at], dst_ref=got_scaled.at[d, at],
            send_sem=ysc_s.at[p, g], recv_sem=ysc_r.at[p, g],
            device_id=(dp_peer(p), e), device_id_type=MESH)

    def arrived_scaled(g, p):
        at = pl.ds(g * group_rows, group_rows)
        source = lax.rem(d + ndp - p, ndp)
        return pltpu.make_async_remote_copy(
            src_ref=got_scaled.at[source, at], dst_ref=got_scaled.at[source, at],
            send_sem=ysc_s.at[p, g], recv_sem=ysc_r.at[p, g],
            device_id=(dp_peer(p), e), device_id_type=MESH)

    def across_back(g, p):
        at = pl.ds(g * group_rows, group_rows)
        return pltpu.make_async_remote_copy(
            src_ref=back_part.at[dp_peer(p), at], dst_ref=back_got.at[p - 1, at],
            send_sem=yb_s.at[p, g], recv_sem=yb_r.at[p, g],
            device_id=(dp_peer(p), e), device_id_type=MESH)

    def across_gram(i, p):
        at = (pl.ds(i * tile, tile), pl.ds(0, (i + 1) * tile))
        return pltpu.make_async_remote_copy(
            src_ref=gram_part.at[at], dst_ref=gram_got.at[(p - 1,) + at],
            send_sem=gram_s.at[p, i], recv_sem=gram_r.at[p, i],
            device_id=(dp_peer(p), e), device_id_type=MESH)

    def across_v(p):
        return pltpu.make_async_remote_copy(
            src_ref=v_part, dst_ref=v_got.at[p - 1],
            send_sem=v_s.at[p], recv_sem=v_r.at[p],
            device_id=(dp_peer(p), e), device_id_type=MESH)

    def scaled_rows(j):
        return dot(select[block(j), :], scaled_ref[...]).astype(BF16)

    def grad_rows(j):
        chosen = select[block(j), 0:tokens] + select[block(j), tokens:2 * tokens]
        return dot(chosen, grad_ref[...]).astype(BF16)

    def put_scaled(j):
        send_scaled[block(j), :] = scaled_rows(j)
        scaled_copy(j, ahead(j)).start()

    def put_grad(j):
        send_grad[block(j), :] = grad_rows(j)
        grad_copy(j, ahead(j)).start()

    def members_of(g, body):
        first = g * members
        loop(first + (1 if first == own else 0), first + members, body)

    others(put_scaled)
    members_of(0, put_grad)
    got_scaled[d, 0:cap, :] = scaled_rows(own)
    got_grad[0:cap, :] = grad_rows(own)
    others(lambda j: scaled_copy(j, ahead(j)).wait_recv())
    members_of(1, put_grad)
    for g in range(GROUPS):
        for p in range(1, ndp):
            across_scaled(g, p).start()

    def back_of(g):
        at = slice(g * group_rows, (g + 1) * group_rows)

        def column(i):
            term = dot(got_grad[at, :], weight_ref[pl.ds(pl.multiple_of(i * tile, tile), tile), :],
                       ((1,), (1,))).astype(BF16)
            cols = pl.ds(pl.multiple_of(lax.rem(i, per_part) * tile, tile), tile)
            back_part[lax.div(i, per_part), at, cols] = term

        loop(0, tiles, column)
        for p in range(1, ndp):
            across_back(g, p).start()

    for g in range(GROUPS - 1):
        members_of(g, lambda j: grad_copy(j, ahead(j)).wait_recv())
        if g + 2 < GROUPS:
            members_of(g + 2, put_grad)
        if g < GROUPS - 2:
            back_of(g)
        if g == GROUPS - 3:
            for h in range(GROUPS):
                for p in range(1, ndp):
                    arrived_scaled(h, p).wait_recv()
            for b in range(ndp):
                early_t[b * part:(b + 1) * part, :] = got_scaled[b, 0:split, :].T
                late_t[b * part:(b + 1) * part, :] = got_scaled[b, split:rows, :].T

    for i in range(tiles):
        at = slice(i * tile, (i + 1) * tile)

        def gradient(c):
            cols = pl.ds(pl.multiple_of(c * chunk, chunk), chunk)
            g_ref[at, cols] = dot(early_t[at, :], got_grad[0:split, cols]).astype(BF16)

        def gram(j):
            other = pl.ds(pl.multiple_of(j * tile, tile), tile)
            gram_part[at, other] = dot(g_ref[at, :], g_ref[other, :], ((1,), (1,))).astype(BF16)

        loop(0, width // chunk, gradient)
        loop(0, i + 1, gram)
        for p in range(1, ndp):
            across_gram(i, p).start()
    back_of(GROUPS - 2)

    def give_back(g):
        at = slice(g * group_rows, (g + 1) * group_rows)
        for p in range(1, ndp):
            across_back(g, p).wait_recv()
        total = back_part[d, at, :].astype(F32)
        for p in range(1, ndp):
            total = total + back_got[p - 1, at, :].astype(F32)
        summed[at, :] = total.astype(BF16)
        members_of(g, lambda j: return_copy(j, behind(j)).start())

    members_of(GROUPS - 1, lambda j: grad_copy(j, ahead(j)).wait_recv())

    def halfway(i):
        at = pl.ds(pl.multiple_of(i * tile, tile), tile)

        def piece(c):
            cols = pl.ds(pl.multiple_of(c * chunk, chunk), chunk)
            late = dot(late_t[at, :], got_grad[split:rows, cols])
            g_ref[at, cols] = (g_ref[at, cols].astype(F32) + 0.5 * late).astype(BF16)

        loop(0, width // chunk, piece)
        v_part[:, at] = dot(got_grad[split:rows, :], g_ref[at, :], ((1,), (1,))).astype(BF16)

    loop(0, tiles, halfway)
    for p in range(1, ndp):
        across_v(p).start()
    for g in range(GROUPS - 2):
        give_back(g)
    back_of(GROUPS - 1)
    give_back(GROUPS - 2)

    def whole(i):
        at = pl.ds(pl.multiple_of(i * tile, tile), tile)

        def piece(c):
            cols = pl.ds(pl.multiple_of(c * chunk, chunk), chunk)
            g_ref[at, cols] = (
                dot(early_t[at, :], got_grad[0:split, cols]) + dot(late_t[at, :], got_grad[split:rows, cols])
            ).astype(BF16)

        loop(0, width // chunk, piece)

    loop(0, tiles, whole)
    for p in range(1, ndp):
        across_v(p).wait_recv()
    v = v_part[...].astype(F32)
    for p in range(1, ndp):
        v = v + v_got[p - 1].astype(F32)
    v_sum = v.astype(BF16)
    for i in range(tiles):
        at = slice(i * tile, (i + 1) * tile)
        gram_sum[at, :] = dot(late_t[at, :], v_sum)
    give_back(GROUPS - 1)
    returned[own * cap:(own + 1) * cap, :] = summed[own * cap:(own + 1) * cap, :]

    squares = jnp.zeros((1, 1), F32)
    for i in range(tiles):
        at = slice(i * tile, (i + 1) * tile)
        for p in range(1, ndp):
            across_gram(i, p).wait_recv()
        for j in range(i + 1):
            other = slice(j * tile, (j + 1) * tile)
            total = gram_part[at, other].astype(F32)
            for p in range(1, ndp):
                total = total + gram_got[p - 1, at, other].astype(F32)
            total = total + gram_sum[at, other] + gram_sum[other, at].T
            gram_sum[at, other] = total
            here = jnp.sum(jnp.sum(total * total, axis=0, keepdims=True), axis=1, keepdims=True)
            squares = squares + here * (1.0 if i == j else 2.0)
    norm_sq = jnp.sqrt(squares) + 1e-6
    inverse = 1.0 / norm_sq
    scale = lax.rsqrt(norm_sq) * (D**0.5)
    c_ref[...] = jnp.broadcast_to(2.25 * scale, c_ref.shape)
    for i in range(tiles):
        at = slice(i * tile, (i + 1) * tile)
        for j in range(i + 1):
            other = slice(j * tile, (j + 1) * tile)
            value = gram_sum[at, other] * inverse
            a_ref[at, other] = value.astype(BF16)
            if j < i:
                a_ref[other, at] = value.T.astype(BF16)

    for p in range(1, ndp):
        for i in range(tiles):
            across_gram(i, p).wait_send()
    a2_ref, w_ref = gram_part, gram_got.at[0]

    def square(i):
        at = pl.ds(pl.multiple_of(i * tile, tile), tile)
        a2 = dot(a_ref[at, :], a_ref[...])
        a1 = a_ref[at, :].astype(F32)
        a2_ref[at, :] = a2.astype(BF16)
        w_ref[at, :] = (1.125 * a1 - 0.125 * a2).astype(BF16)
        gram_sum[at, :] = 1.6875 * a2 - 2.4375 * a1

    def finish(i):
        at = pl.ds(pl.multiple_of(i * tile, tile), tile)
        last = dot(a2_ref[at, :], w_ref[...])
        p_ref[at, :] = ((gram_sum[at, :] - 0.5 * last) * scale).astype(BF16)

    loop(0, tiles, square)
    loop(0, tiles, finish)

    others(lambda j: return_copy(j, behind(j)).wait_recv())
    step = min(256, tokens)
    for k in range(2):
        for t in range(0, tokens, step):
            cols = slice(k * tokens + t, k * tokens + t + step)
            value = dot(select[:, cols], returned[...], ((0,), (0,)))
            picked_ref[k, t:t + step, :] = (prob_ref[t:t + step, k:k + 1] * value).astype(BF16)

    def drain(j):
        scaled_copy(j, ahead(j)).wait_send()
        grad_copy(j, ahead(j)).wait_send()
        return_copy(j, behind(j)).wait_send()

    others(drain)
    for p in range(1, ndp):
        for g in range(GROUPS):
            across_scaled(g, p).wait_send()
            across_back(g, p).wait_send()
        across_v(p).wait_send()


def per_device(n, ndp, grad_out, hidden, gate_prob, expert_ids, weights):
    tokens, width = grad_out.shape
    top = expert_ids.shape[1]
    part = hidden.shape[2]
    hid = part * ndp
    capacity = 5 * tokens * top // (4 * n)
    cap = -(-capacity // 16) * 16
    rows = n * cap
    late = rows // GROUPS
    tiles = hid // min(256, part)
    scaled = (gate_prob[:, :, None] * hidden.astype(F32)).astype(BF16)
    scaled = scaled.transpose(1, 0, 2).reshape(top * tokens, part)
    vmem = pl.BlockSpec(memory_space=pltpu.VMEM)
    dma = pltpu.SemaphoreType.DMA
    grads, poly, scale, picked = pl.pallas_call(
        functools.partial(kernel, n, ndp, cap),
        out_shape=[
            jax.ShapeDtypeStruct((hid, width), BF16),
            jax.ShapeDtypeStruct((hid, hid), BF16),
            jax.ShapeDtypeStruct((8, 128), F32),
            jax.ShapeDtypeStruct((top, tokens, part), BF16),
        ],
        in_specs=[vmem] * 5,
        out_specs=[vmem] * 4,
        scratch_shapes=[
            pltpu.VMEM((n, tokens), F32),
            pltpu.VMEM((n, tokens), F32),
            pltpu.VMEM((rows, top * tokens), BF16),
            pltpu.VMEM((rows, width), BF16),
            pltpu.VMEM((rows, width), BF16),
            pltpu.VMEM((rows, part), BF16),
            pltpu.VMEM((ndp, rows, part), BF16),
            pltpu.VMEM((hid, rows - late), BF16),
            pltpu.VMEM((hid, late), BF16),
            pltpu.VMEM((ndp, rows, part), BF16),
            pltpu.VMEM((ndp - 1, rows, part), BF16),
            pltpu.VMEM((rows, part), BF16),
            pltpu.VMEM((rows, part), BF16),
            pltpu.VMEM((hid, hid), BF16),
            pltpu.VMEM((ndp - 1, hid, hid), BF16),
            pltpu.VMEM((late, hid), BF16),
            pltpu.VMEM((ndp - 1, late, hid), BF16),
            pltpu.VMEM((hid, hid), F32),
            pltpu.VMEM((hid, hid), BF16),
        ] + [dma((n,))] * 6 + [dma((ndp, GROUPS))] * 4 + [dma((ndp, tiles))] * 2 + [dma((ndp,))] * 2,
        compiler_params=pltpu.CompilerParams(
            collective_id=0, has_side_effects=True, vmem_limit_bytes=62 * 1024 * 1024
        ),
        cost_estimate=pl.CostEstimate(flops=20_000_000_000, bytes_accessed=16_000_000, transcendentals=0),
    )(expert_ids.T, gate_prob, grad_out, scaled, weights[0])
    update = dot(poly, grads) + grads.astype(F32) * scale[0, 0]
    hidden_grad = picked.transpose(1, 0, 2)
    return (hidden_grad, update[None])


def solution(mesh):
    in_specs = (
        P("expert", "dp"),
        P("expert", None, "dp"),
        P("expert", None),
        P("expert", None),
        P("expert", None, "dp"),
    )
    out_specs = (P("expert", None, "dp"), P("expert", None, "dp"))
    return jax.shard_map(
        functools.partial(per_device, mesh.shape["expert"], mesh.shape["dp"]),
        mesh=mesh, in_specs=in_specs, out_specs=out_specs, check_vma=False,
    )
```

```python
import functools

import jax
import jax.numpy as jnp
from jax import lax
from jax.experimental import pallas as pl
from jax.experimental.pallas import tpu as pltpu
from jax.sharding import PartitionSpec as P

D = 4096
MESH = pl.DeviceIdType.MESH
BF16 = jnp.bfloat16
F32 = jnp.float32
GROUPS = 4


def dot(a, b, dims=((1,), (0,))):
    return lax.dot_general(a, b, (dims, ((), ())), preferred_element_type=F32)


def kernel(
    n, ndp, cap,
    ids_ref, prob_ref, grad_ref, scaled_ref, weight_ref,
    g_ref, p_ref, c_ref, picked_ref,
    rank0, rank1, select, send_grad, got_grad, send_scaled, got_scaled, early_t, late_t,
    back_part, back_got, summed, returned,
    gram_part, gram_got, v_part, v_got, gram_sum, a_ref,
    grad_s, grad_r, sc_s, sc_r, ret_s, ret_r, ysc_s, ysc_r, yb_s, yb_r, gram_s, gram_r, v_s, v_r,
):
    d, e = lax.axis_index("dp"), lax.axis_index("expert")
    tokens, width = grad_ref.shape
    rows = n * cap
    part = scaled_ref.shape[1]
    hid = part * ndp
    tile = min(256, part)
    tiles, per_part = hid // tile, part // tile
    own = 0
    members = n // GROUPS
    group_rows = members * cap
    chunk = min(512, width)
    split = rows - group_rows

    def block(j):
        return pl.ds(pl.multiple_of(j * cap, 16), cap)

    def offset(j):
        return lax.rem(j, members) * GROUPS + lax.div(j, members)

    def ahead(j):
        return lax.rem(e + offset(j), n)

    def behind(j):
        return lax.rem(e + n - offset(j), n)

    def loop(lo, hi, body):
        def step(i, carry):
            body(i)
            return carry
        lax.fori_loop(lo, hi, step, 0)

    def others(body):
        loop(1, n, body)

    def dp_peer(p):
        return lax.rem(d + p, ndp)

    barrier = pltpu.get_barrier_semaphore()

    def greet(j):
        pl.semaphore_signal(barrier, inc=1, device_id=(d, ahead(j)), device_id_type=MESH)

    others(greet)
    for p in range(1, ndp):
        pl.semaphore_signal(barrier, inc=1, device_id=(dp_peer(p), e), device_id_type=MESH)

    expert_row = lax.broadcasted_iota(jnp.int32, (n, tokens), 0)
    is0 = ids_ref[0:1, :] == expert_row
    is1 = ids_ref[1:2, :] == expert_row
    named = (jnp.where(is0, 1.0, 0.0) + jnp.where(is1, 1.0, 0.0)).astype(BF16)
    earlier = lax.broadcasted_iota(jnp.int32, (tokens, tokens), 0) < lax.broadcasted_iota(
        jnp.int32, (tokens, tokens), 1
    )
    rank = dot(named, jnp.where(earlier, 1.0, 0.0).astype(BF16))
    rank0[...] = jnp.where(is0, rank, -1.0)
    rank1[...] = jnp.where(is1, rank, -1.0)

    def build(j):
        to = ahead(j)
        slot = lax.broadcasted_iota(jnp.int32, (cap, tokens), 0).astype(F32)
        for k, ref in ((0, rank0), (1, rank1)):
            select[block(j), k * tokens:(k + 1) * tokens] = jnp.where(
                ref[pl.ds(to, 1), :] == slot, 1.0, 0.0
            ).astype(BF16)

    loop(0, n, build)
    pl.semaphore_wait(barrier, n - 1 + ndp - 1)

    def scaled_copy(j, peer):
        return pltpu.make_async_remote_copy(
            src_ref=send_scaled.at[block(j)], dst_ref=got_scaled.at[d, block(j)],
            send_sem=sc_s.at[j], recv_sem=sc_r.at[j], device_id=(d, peer), device_id_type=MESH)

    def grad_copy(j, peer):
        return pltpu.make_async_remote_copy(
            src_ref=send_grad.at[block(j)], dst_ref=got_grad.at[block(j)],
            send_sem=grad_s.at[j], recv_sem=grad_r.at[j], device_id=(d, peer), device_id_type=MESH)

    def return_copy(j, peer):
        return pltpu.make_async_remote_copy(
            src_ref=summed.at[block(j)], dst_ref=returned.at[block(j)],
            send_sem=ret_s.at[j], recv_sem=ret_r.at[j], device_id=(d, peer), device_id_type=MESH)

    def across_scaled(g, p):
        at = pl.ds(g * group_rows, group_rows)
        return pltpu.make_async_remote_copy(
            src_ref=got_scaled.at[d, at], dst_ref=got_scaled.at[d, at],
            send_sem=ysc_s.at[p, g], recv_sem=ysc_r.at[p, g],
            device_id=(dp_peer(p), e), device_id_type=MESH)

    def arrived_scaled(g, p):
        at = pl.ds(g * group_rows, group_rows)
        source = lax.rem(d + ndp - p, ndp)
        return pltpu.make_async_remote_copy(
            src_ref=got_scaled.at[source, at], dst_ref=got_scaled.at[source, at],
            send_sem=ysc_s.at[p, g], recv_sem=ysc_r.at[p, g],
            device_id=(dp_peer(p), e), device_id_type=MESH)

    def across_back(g, p):
        at = pl.ds(g * group_rows, group_rows)
        return pltpu.make_async_remote_copy(
            src_ref=back_part.at[dp_peer(p), at], dst_ref=back_got.at[p - 1, at],
            send_sem=yb_s.at[p, g], recv_sem=yb_r.at[p, g],
            device_id=(dp_peer(p), e), device_id_type=MESH)

    def across_gram(i, p):
        at = (pl.ds(i * tile, tile), pl.ds(0, (i + 1) * tile))
        return pltpu.make_async_remote_copy(
            src_ref=gram_part.at[at], dst_ref=gram_got.at[(p - 1,) + at],
            send_sem=gram_s.at[p, i], recv_sem=gram_r.at[p, i],
            device_id=(dp_peer(p), e), device_id_type=MESH)

    def across_v(p):
        return pltpu.make_async_remote_copy(
            src_ref=v_part, dst_ref=v_got.at[p - 1],
            send_sem=v_s.at[p], recv_sem=v_r.at[p],
            device_id=(dp_peer(p), e), device_id_type=MESH)

    def scaled_rows(j):
        return dot(select[block(j), :], scaled_ref[...]).astype(BF16)

    def grad_rows(j):
        chosen = select[block(j), 0:tokens] + select[block(j), tokens:2 * tokens]
        return dot(chosen, grad_ref[...]).astype(BF16)

    def put_scaled(j):
        send_scaled[block(j), :] = scaled_rows(j)
        scaled_copy(j, ahead(j)).start()

    def put_grad(j):
        send_grad[block(j), :] = grad_rows(j)
        grad_copy(j, ahead(j)).start()

    def members_of(g, body):
        first = g * members
        loop(first + (1 if first == own else 0), first + members, body)

    others(put_scaled)
    others(put_grad)
    got_scaled[d, 0:cap, :] = scaled_rows(own)
    got_grad[0:cap, :] = grad_rows(own)
    others(lambda j: scaled_copy(j, ahead(j)).wait_recv())
    for g in range(GROUPS):
        for p in range(1, ndp):
            across_scaled(g, p).start()

    def back_of(g):
        at = slice(g * group_rows, (g + 1) * group_rows)

        def column(i):
            term = dot(got_grad[at, :], weight_ref[pl.ds(pl.multiple_of(i * tile, tile), tile), :],
                       ((1,), (1,))).astype(BF16)
            cols = pl.ds(pl.multiple_of(lax.rem(i, per_part) * tile, tile), tile)
            back_part[lax.div(i, per_part), at, cols] = term

        loop(0, tiles, column)
        for p in range(1, ndp):
            across_back(g, p).start()

    for g in range(GROUPS - 1):
        members_of(g, lambda j: grad_copy(j, ahead(j)).wait_recv())
        if g < GROUPS - 2:
            back_of(g)
        if g == GROUPS - 3:
            for h in range(GROUPS):
                for p in range(1, ndp):
                    arrived_scaled(h, p).wait_recv()
            for b in range(ndp):
                early_t[b * part:(b + 1) * part, :] = got_scaled[b, 0:split, :].T
                late_t[b * part:(b + 1) * part, :] = got_scaled[b, split:rows, :].T

    for i in range(tiles):
        at = slice(i * tile, (i + 1) * tile)

        def gradient(c):
            cols = pl.ds(pl.multiple_of(c * chunk, chunk), chunk)
            g_ref[at, cols] = dot(early_t[at, :], got_grad[0:split, cols]).astype(BF16)

        def gram(j):
            other = pl.ds(pl.multiple_of(j * tile, tile), tile)
            gram_part[at, other] = dot(g_ref[at, :], g_ref[other, :], ((1,), (1,))).astype(BF16)

        loop(0, width // chunk, gradient)
        loop(0, i + 1, gram)
        for p in range(1, ndp):
            across_gram(i, p).start()
    back_of(GROUPS - 2)

    def give_back(g):
        at = slice(g * group_rows, (g + 1) * group_rows)
        for p in range(1, ndp):
            across_back(g, p).wait_recv()
        total = back_part[d, at, :].astype(F32)
        for p in range(1, ndp):
            total = total + back_got[p - 1, at, :].astype(F32)
        summed[at, :] = total.astype(BF16)
        members_of(g, lambda j: return_copy(j, behind(j)).start())

    members_of(GROUPS - 1, lambda j: grad_copy(j, ahead(j)).wait_recv())

    def halfway(i):
        at = pl.ds(pl.multiple_of(i * tile, tile), tile)

        def piece(c):
            cols = pl.ds(pl.multiple_of(c * chunk, chunk), chunk)
            late = dot(late_t[at, :], got_grad[split:rows, cols])
            g_ref[at, cols] = (g_ref[at, cols].astype(F32) + 0.5 * late).astype(BF16)

        loop(0, width // chunk, piece)
        v_part[:, at] = dot(got_grad[split:rows, :], g_ref[at, :], ((1,), (1,))).astype(BF16)

    loop(0, tiles, halfway)
    for p in range(1, ndp):
        across_v(p).start()
    for g in range(GROUPS - 2):
        give_back(g)
    back_of(GROUPS - 1)
    give_back(GROUPS - 2)

    def whole(i):
        at = pl.ds(pl.multiple_of(i * tile, tile), tile)

        def piece(c):
            cols = pl.ds(pl.multiple_of(c * chunk, chunk), chunk)
            g_ref[at, cols] = (
                dot(early_t[at, :], got_grad[0:split, cols]) + dot(late_t[at, :], got_grad[split:rows, cols])
            ).astype(BF16)

        loop(0, width // chunk, piece)

    loop(0, tiles, whole)
    for p in range(1, ndp):
        across_v(p).wait_recv()
    v = v_part[...].astype(F32)
    for p in range(1, ndp):
        v = v + v_got[p - 1].astype(F32)
    v_sum = v.astype(BF16)
    for i in range(tiles):
        at = slice(i * tile, (i + 1) * tile)
        gram_sum[at, :] = dot(late_t[at, :], v_sum)
    give_back(GROUPS - 1)
    returned[own * cap:(own + 1) * cap, :] = summed[own * cap:(own + 1) * cap, :]

    squares = jnp.zeros((1, 1), F32)
    for i in range(tiles):
        at = slice(i * tile, (i + 1) * tile)
        for p in range(1, ndp):
            across_gram(i, p).wait_recv()
        for j in range(i + 1):
            other = slice(j * tile, (j + 1) * tile)
            total = gram_part[at, other].astype(F32)
            for p in range(1, ndp):
                total = total + gram_got[p - 1, at, other].astype(F32)
            total = total + gram_sum[at, other] + gram_sum[other, at].T
            gram_sum[at, other] = total
            here = jnp.sum(jnp.sum(total * total, axis=0, keepdims=True), axis=1, keepdims=True)
            squares = squares + here * (1.0 if i == j else 2.0)
    norm_sq = jnp.sqrt(squares) + 1e-6
    inverse = 1.0 / norm_sq
    scale = lax.rsqrt(norm_sq) * (D**0.5)
    c_ref[...] = jnp.broadcast_to(2.25 * scale, c_ref.shape)
    for i in range(tiles):
        at = slice(i * tile, (i + 1) * tile)
        for j in range(i + 1):
            other = slice(j * tile, (j + 1) * tile)
            value = gram_sum[at, other] * inverse
            a_ref[at, other] = value.astype(BF16)
            if j < i:
                a_ref[other, at] = value.T.astype(BF16)

    for p in range(1, ndp):
        for i in range(tiles):
            across_gram(i, p).wait_send()
    a2_ref, w_ref = gram_part, gram_got.at[0]

    def square(i):
        at = pl.ds(pl.multiple_of(i * tile, tile), tile)
        a2 = dot(a_ref[at, :], a_ref[...])
        a1 = a_ref[at, :].astype(F32)
        a2_ref[at, :] = a2.astype(BF16)
        w_ref[at, :] = (1.125 * a1 - 0.125 * a2).astype(BF16)
        gram_sum[at, :] = 1.6875 * a2 - 2.4375 * a1

    def finish(i):
        at = pl.ds(pl.multiple_of(i * tile, tile), tile)
        last = dot(a2_ref[at, :], w_ref[...])
        p_ref[at, :] = ((gram_sum[at, :] - 0.5 * last) * scale).astype(BF16)

    loop(0, tiles, square)
    loop(0, tiles, finish)

    others(lambda j: return_copy(j, behind(j)).wait_recv())
    step = min(256, tokens)
    for k in range(2):
        for t in range(0, tokens, step):
            cols = slice(k * tokens + t, k * tokens + t + step)
            value = dot(select[:, cols], returned[...], ((0,), (0,)))
            picked_ref[k, t:t + step, :] = (prob_ref[t:t + step, k:k + 1] * value).astype(BF16)

    def drain(j):
        scaled_copy(j, ahead(j)).wait_send()
        grad_copy(j, ahead(j)).wait_send()
        return_copy(j, behind(j)).wait_send()

    others(drain)
    for p in range(1, ndp):
        for g in range(GROUPS):
            across_scaled(g, p).wait_send()
            across_back(g, p).wait_send()
        across_v(p).wait_send()


def update_kernel(c_ref, p_ref, g_ref, out_ref):
    grads = g_ref[...]
    out_ref[...] = dot(p_ref[...], grads) + grads.astype(F32) * c_ref[0:1, 0:1]


def per_device(n, ndp, grad_out, hidden, gate_prob, expert_ids, weights):
    tokens, width = grad_out.shape
    top = expert_ids.shape[1]
    part = hidden.shape[2]
    hid = part * ndp
    capacity = 5 * tokens * top // (4 * n)
    cap = -(-capacity // 16) * 16
    rows = n * cap
    late = rows // GROUPS
    tiles = hid // min(256, part)
    scaled = (gate_prob[:, :, None] * hidden.astype(F32)).astype(BF16)
    scaled = scaled.transpose(1, 0, 2).reshape(top * tokens, part)
    vmem = pl.BlockSpec(memory_space=pltpu.VMEM)
    dma = pltpu.SemaphoreType.DMA
    grads, poly, scale, picked = pl.pallas_call(
        functools.partial(kernel, n, ndp, cap),
        out_shape=[
            jax.ShapeDtypeStruct((hid, width), BF16),
            jax.ShapeDtypeStruct((hid, hid), BF16),
            jax.ShapeDtypeStruct((8, 128), F32),
            jax.ShapeDtypeStruct((top, tokens, part), BF16),
        ],
        in_specs=[vmem] * 5,
        out_specs=[vmem] * 4,
        scratch_shapes=[
            pltpu.VMEM((n, tokens), F32),
            pltpu.VMEM((n, tokens), F32),
            pltpu.VMEM((rows, top * tokens), BF16),
            pltpu.VMEM((rows, width), BF16),
            pltpu.VMEM((rows, width), BF16),
            pltpu.VMEM((rows, part), BF16),
            pltpu.VMEM((ndp, rows, part), BF16),
            pltpu.VMEM((hid, rows - late), BF16),
            pltpu.VMEM((hid, late), BF16),
            pltpu.VMEM((ndp, rows, part), BF16),
            pltpu.VMEM((ndp - 1, rows, part), BF16),
            pltpu.VMEM((rows, part), BF16),
            pltpu.VMEM((rows, part), BF16),
            pltpu.VMEM((hid, hid), BF16),
            pltpu.VMEM((ndp - 1, hid, hid), BF16),
            pltpu.VMEM((late, hid), BF16),
            pltpu.VMEM((ndp - 1, late, hid), BF16),
            pltpu.VMEM((hid, hid), F32),
            pltpu.VMEM((hid, hid), BF16),
        ] + [dma((n,))] * 6 + [dma((ndp, GROUPS))] * 4 + [dma((ndp, tiles))] * 2 + [dma((ndp,))] * 2,
        compiler_params=pltpu.CompilerParams(
            collective_id=0, has_side_effects=True, vmem_limit_bytes=62 * 1024 * 1024
        ),
        cost_estimate=pl.CostEstimate(flops=20_000_000_000, bytes_accessed=16_000_000, transcendentals=0),
    )(expert_ids.T, gate_prob, grad_out, scaled, weights[0])
    chunk = min(256, width)
    update = pl.pallas_call(
        update_kernel,
        grid=(width // chunk,),
        out_shape=jax.ShapeDtypeStruct((hid, width), F32),
        in_specs=[
            pl.BlockSpec((8, 128), lambda c: (0, 0)),
            pl.BlockSpec((hid, hid), lambda c: (0, 0)),
            pl.BlockSpec((hid, chunk), lambda c: (0, c)),
        ],
        out_specs=pl.BlockSpec((hid, chunk), lambda c: (0, c)),
        compiler_params=pltpu.CompilerParams(vmem_limit_bytes=24 * 1024 * 1024),
        cost_estimate=pl.CostEstimate(
            flops=2 * hid * hid * width, bytes_accessed=6 * hid * width, transcendentals=0),
    )(scale, poly, grads)
    hidden_grad = picked.transpose(1, 0, 2)
    return (hidden_grad, update[None])


def solution(mesh):
    in_specs = (
        P("expert", "dp"),
        P("expert", None, "dp"),
        P("expert", None),
        P("expert", None),
        P("expert", None, "dp"),
    )
    out_specs = (P("expert", None, "dp"), P("expert", None, "dp"))
    return jax.shard_map(
        functools.partial(per_device, mesh.shape["expert"], mesh.shape["dp"]),
        mesh=mesh, in_specs=in_specs, out_specs=out_specs, check_vma=False,
    )
```

```python
import functools

import jax
import jax.numpy as jnp
from jax import lax
from jax.experimental import pallas as pl
from jax.experimental.pallas import tpu as pltpu
from jax.sharding import PartitionSpec as P

D = 4096
MESH = pl.DeviceIdType.MESH
BF16 = jnp.bfloat16
F32 = jnp.float32
GROUPS = 4


def dot(a, b, dims=((1,), (0,))):
    return lax.dot_general(a, b, (dims, ((), ())), preferred_element_type=F32)


def kernel(
    n, ndp, cap,
    ids_ref, prob_ref, grad_ref, scaled_ref, weight_ref,
    g_ref, p_ref, c_ref, picked_ref,
    rank0, rank1, select, send_grad, got_grad, send_scaled, got_scaled, early_t, late_t,
    back_part, back_got, summed, returned,
    gram_part, gram_got, v_part, v_got, gram_sum, a_ref,
    grad_s, grad_r, sc_s, sc_r, ret_s, ret_r, ysc_s, ysc_r, yb_s, yb_r, gram_s, gram_r, v_s, v_r,
):
    d, e = lax.axis_index("dp"), lax.axis_index("expert")
    tokens, width = grad_ref.shape
    rows = n * cap
    part = scaled_ref.shape[1]
    hid = part * ndp
    tile = min(256, part)
    tiles, per_part = hid // tile, part // tile
    own = 0
    members = n // GROUPS
    group_rows = members * cap
    chunk = min(512, width)
    split = rows - group_rows

    def block(j):
        return pl.ds(pl.multiple_of(j * cap, 16), cap)

    def offset(j):
        return lax.rem(j, members) * GROUPS + lax.div(j, members)

    def ahead(j):
        return lax.rem(e + offset(j), n)

    def behind(j):
        return lax.rem(e + n - offset(j), n)

    def loop(lo, hi, body):
        def step(i, carry):
            body(i)
            return carry
        lax.fori_loop(lo, hi, step, 0)

    def others(body):
        loop(1, n, body)

    def dp_peer(p):
        return lax.rem(d + p, ndp)

    barrier = pltpu.get_barrier_semaphore()

    def greet(j):
        pl.semaphore_signal(barrier, inc=1, device_id=(d, ahead(j)), device_id_type=MESH)

    others(greet)
    for p in range(1, ndp):
        pl.semaphore_signal(barrier, inc=1, device_id=(dp_peer(p), e), device_id_type=MESH)

    expert_row = lax.broadcasted_iota(jnp.int32, (n, tokens), 0)
    is0 = ids_ref[0:1, :] == expert_row
    is1 = ids_ref[1:2, :] == expert_row
    named = (jnp.where(is0, 1.0, 0.0) + jnp.where(is1, 1.0, 0.0)).astype(BF16)
    earlier = lax.broadcasted_iota(jnp.int32, (tokens, tokens), 0) < lax.broadcasted_iota(
        jnp.int32, (tokens, tokens), 1
    )
    rank = dot(named, jnp.where(earlier, 1.0, 0.0).astype(BF16))
    rank0[...] = jnp.where(is0, rank, -1.0)
    rank1[...] = jnp.where(is1, rank, -1.0)

    def build(j):
        to = ahead(j)
        slot = lax.broadcasted_iota(jnp.int32, (cap, tokens), 0).astype(F32)
        for k, ref in ((0, rank0), (1, rank1)):
            select[block(j), k * tokens:(k + 1) * tokens] = jnp.where(
                ref[pl.ds(to, 1), :] == slot, 1.0, 0.0
            ).astype(BF16)

    loop(0, n, build)
    pl.semaphore_wait(barrier, n - 1 + ndp - 1)

    def scaled_copy(j, peer):
        return pltpu.make_async_remote_copy(
            src_ref=send_scaled.at[block(j)], dst_ref=got_scaled.at[d, block(j)],
            send_sem=sc_s.at[j], recv_sem=sc_r.at[j], device_id=(d, peer), device_id_type=MESH)

    def grad_copy(j, peer):
        return pltpu.make_async_remote_copy(
            src_ref=send_grad.at[block(j)], dst_ref=got_grad.at[block(j)],
            send_sem=grad_s.at[j], recv_sem=grad_r.at[j], device_id=(d, peer), device_id_type=MESH)

    def return_copy(j, peer):
        return pltpu.make_async_remote_copy(
            src_ref=summed.at[block(j)], dst_ref=returned.at[block(j)],
            send_sem=ret_s.at[j], recv_sem=ret_r.at[j], device_id=(d, peer), device_id_type=MESH)

    def across_scaled(g, p):
        at = pl.ds(g * group_rows, group_rows)
        return pltpu.make_async_remote_copy(
            src_ref=got_scaled.at[d, at], dst_ref=got_scaled.at[d, at],
            send_sem=ysc_s.at[p, g], recv_sem=ysc_r.at[p, g],
            device_id=(dp_peer(p), e), device_id_type=MESH)

    def arrived_scaled(g, p):
        at = pl.ds(g * group_rows, group_rows)
        source = lax.rem(d + ndp - p, ndp)
        return pltpu.make_async_remote_copy(
            src_ref=got_scaled.at[source, at], dst_ref=got_scaled.at[source, at],
            send_sem=ysc_s.at[p, g], recv_sem=ysc_r.at[p, g],
            device_id=(dp_peer(p), e), device_id_type=MESH)

    def across_back(g, p):
        at = pl.ds(g * group_rows, group_rows)
        return pltpu.make_async_remote_copy(
            src_ref=back_part.at[dp_peer(p), at], dst_ref=back_got.at[p - 1, at],
            send_sem=yb_s.at[p, g], recv_sem=yb_r.at[p, g],
            device_id=(dp_peer(p), e), device_id_type=MESH)

    def across_gram(i, p):
        at = (pl.ds(i * tile, tile), pl.ds(0, (i + 1) * tile))
        return pltpu.make_async_remote_copy(
            src_ref=gram_part.at[at], dst_ref=gram_got.at[(p - 1,) + at],
            send_sem=gram_s.at[p, i], recv_sem=gram_r.at[p, i],
            device_id=(dp_peer(p), e), device_id_type=MESH)

    def across_v(p):
        return pltpu.make_async_remote_copy(
            src_ref=v_part, dst_ref=v_got.at[p - 1],
            send_sem=v_s.at[p], recv_sem=v_r.at[p],
            device_id=(dp_peer(p), e), device_id_type=MESH)

    def scaled_rows(j):
        return dot(select[block(j), :], scaled_ref[...]).astype(BF16)

    def grad_rows(j):
        chosen = select[block(j), 0:tokens] + select[block(j), tokens:2 * tokens]
        return dot(chosen, grad_ref[...]).astype(BF16)

    def put_scaled(j):
        send_scaled[block(j), :] = scaled_rows(j)
        scaled_copy(j, ahead(j)).start()

    def put_grad(j):
        send_grad[block(j), :] = grad_rows(j)
        grad_copy(j, ahead(j)).start()

    def members_of(g, body):
        first = g * members
        loop(first + (1 if first == own else 0), first + members, body)

    others(put_scaled)
    window = members * 3 // 2
    first_stop = window + members
    stops = (first_stop, first_stop + members, n)

    def put_later(j):
        send_grad[block(j), :] = grad_rows(j)
        grad_copy(j - window, ahead(j - window)).wait_send()
        grad_copy(j, ahead(j)).start()

    loop(1, window + 1, put_grad)
    got_scaled[d, 0:cap, :] = scaled_rows(own)
    got_grad[0:cap, :] = grad_rows(own)
    others(lambda j: scaled_copy(j, ahead(j)).wait_recv())
    for g in range(GROUPS):
        for p in range(1, ndp):
            across_scaled(g, p).start()

    def back_of(g):
        at = slice(g * group_rows, (g + 1) * group_rows)

        def column(i):
            term = dot(got_grad[at, :], weight_ref[pl.ds(pl.multiple_of(i * tile, tile), tile), :],
                       ((1,), (1,))).astype(BF16)
            cols = pl.ds(pl.multiple_of(lax.rem(i, per_part) * tile, tile), tile)
            back_part[lax.div(i, per_part), at, cols] = term

        loop(0, tiles, column)
        for p in range(1, ndp):
            across_back(g, p).start()

    for g in range(GROUPS - 1):
        loop(window + 1 if g == 0 else stops[g - 1], stops[g], put_later)
        members_of(g, lambda j: grad_copy(j, ahead(j)).wait_recv())
        if g < GROUPS - 2:
            back_of(g)
        if g == GROUPS - 3:
            for h in range(GROUPS):
                for p in range(1, ndp):
                    arrived_scaled(h, p).wait_recv()
            for b in range(ndp):
                early_t[b * part:(b + 1) * part, :] = got_scaled[b, 0:split, :].T
                late_t[b * part:(b + 1) * part, :] = got_scaled[b, split:rows, :].T

    for i in range(tiles):
        at = slice(i * tile, (i + 1) * tile)

        def gradient(c):
            cols = pl.ds(pl.multiple_of(c * chunk, chunk), chunk)
            g_ref[at, cols] = dot(early_t[at, :], got_grad[0:split, cols]).astype(BF16)

        def gram(j):
            other = pl.ds(pl.multiple_of(j * tile, tile), tile)
            gram_part[at, other] = dot(g_ref[at, :], g_ref[other, :], ((1,), (1,))).astype(BF16)

        loop(0, width // chunk, gradient)
        loop(0, i + 1, gram)
        for p in range(1, ndp):
            across_gram(i, p).start()
    back_of(GROUPS - 2)

    def give_back(g):
        at = slice(g * group_rows, (g + 1) * group_rows)
        for p in range(1, ndp):
            across_back(g, p).wait_recv()
        total = back_part[d, at, :].astype(F32)
        for p in range(1, ndp):
            total = total + back_got[p - 1, at, :].astype(F32)
        summed[at, :] = total.astype(BF16)
        members_of(g, lambda j: return_copy(j, behind(j)).start())

    members_of(GROUPS - 1, lambda j: grad_copy(j, ahead(j)).wait_recv())

    back_of(GROUPS - 1)

    def halfway(i):
        at = pl.ds(pl.multiple_of(i * tile, tile), tile)

        def piece(c):
            cols = pl.ds(pl.multiple_of(c * chunk, chunk), chunk)
            late = dot(late_t[at, :], got_grad[split:rows, cols])
            g_ref[at, cols] = (g_ref[at, cols].astype(F32) + 0.5 * late).astype(BF16)

        loop(0, width // chunk, piece)
        v_part[:, at] = dot(got_grad[split:rows, :], g_ref[at, :], ((1,), (1,))).astype(BF16)

    loop(0, tiles, halfway)
    for p in range(1, ndp):
        across_v(p).start()
    for g in range(GROUPS - 1):
        give_back(g)

    def whole(i):
        at = pl.ds(pl.multiple_of(i * tile, tile), tile)

        def piece(c):
            cols = pl.ds(pl.multiple_of(c * chunk, chunk), chunk)
            g_ref[at, cols] = (
                dot(early_t[at, :], got_grad[0:split, cols]) + dot(late_t[at, :], got_grad[split:rows, cols])
            ).astype(BF16)

        loop(0, width // chunk, piece)

    loop(0, tiles, whole)
    give_back(GROUPS - 1)
    for p in range(1, ndp):
        across_v(p).wait_recv()
    v = v_part[...].astype(F32)
    for p in range(1, ndp):
        v = v + v_got[p - 1].astype(F32)
    v_sum = v.astype(BF16)
    for i in range(tiles):
        at = slice(i * tile, (i + 1) * tile)
        gram_sum[at, :] = dot(late_t[at, :], v_sum)
    returned[own * cap:(own + 1) * cap, :] = summed[own * cap:(own + 1) * cap, :]

    squares = jnp.zeros((1, 1), F32)
    for i in range(tiles):
        at = slice(i * tile, (i + 1) * tile)
        for p in range(1, ndp):
            across_gram(i, p).wait_recv()
        for j in range(i + 1):
            other = slice(j * tile, (j + 1) * tile)
            total = gram_part[at, other].astype(F32)
            for p in range(1, ndp):
                total = total + gram_got[p - 1, at, other].astype(F32)
            total = total + gram_sum[at, other] + gram_sum[other, at].T
            gram_sum[at, other] = total
            here = jnp.sum(jnp.sum(total * total, axis=0, keepdims=True), axis=1, keepdims=True)
            squares = squares + here * (1.0 if i == j else 2.0)
    norm_sq = jnp.sqrt(squares) + 1e-6
    inverse = 1.0 / norm_sq
    scale = lax.rsqrt(norm_sq) * (D**0.5)
    c_ref[...] = jnp.broadcast_to(2.25 * scale, c_ref.shape)
    for i in range(tiles):
        at = slice(i * tile, (i + 1) * tile)
        for j in range(i + 1):
            other = slice(j * tile, (j + 1) * tile)
            value = gram_sum[at, other] * inverse
            a_ref[at, other] = value.astype(BF16)
            if j < i:
                a_ref[other, at] = value.T.astype(BF16)

    for p in range(1, ndp):
        for i in range(tiles):
            across_gram(i, p).wait_send()
    a2_ref, w_ref = gram_part, gram_got.at[0]

    def square(i):
        at = pl.ds(pl.multiple_of(i * tile, tile), tile)
        a2 = dot(a_ref[at, :], a_ref[...])
        a1 = a_ref[at, :].astype(F32)
        a2_ref[at, :] = a2.astype(BF16)
        w_ref[at, :] = (1.125 * a1 - 0.125 * a2).astype(BF16)
        gram_sum[at, :] = 1.6875 * a2 - 2.4375 * a1

    def finish(i):
        at = pl.ds(pl.multiple_of(i * tile, tile), tile)
        last = dot(a2_ref[at, :], w_ref[...])
        p_ref[at, :] = ((gram_sum[at, :] - 0.5 * last) * scale).astype(BF16)

    loop(0, tiles, square)
    loop(0, tiles, finish)

    others(lambda j: return_copy(j, behind(j)).wait_recv())
    step = min(256, tokens)
    for k in range(2):
        for t in range(0, tokens, step):
            cols = slice(k * tokens + t, k * tokens + t + step)
            value = dot(select[:, cols], returned[...], ((0,), (0,)))
            picked_ref[k, t:t + step, :] = (prob_ref[t:t + step, k:k + 1] * value).astype(BF16)

    def drain(j):
        scaled_copy(j, ahead(j)).wait_send()
        return_copy(j, behind(j)).wait_send()

    others(drain)
    loop(n - window, n, lambda j: grad_copy(j, ahead(j)).wait_send())
    for p in range(1, ndp):
        for g in range(GROUPS):
            across_scaled(g, p).wait_send()
            across_back(g, p).wait_send()
        across_v(p).wait_send()


def update_kernel(c_ref, p_ref, g_ref, out_ref):
    grads = g_ref[...]
    out_ref[...] = dot(p_ref[...], grads) + grads.astype(F32) * c_ref[0:1, 0:1]


def per_device(n, ndp, grad_out, hidden, gate_prob, expert_ids, weights):
    tokens, width = grad_out.shape
    top = expert_ids.shape[1]
    part = hidden.shape[2]
    hid = part * ndp
    capacity = 5 * tokens * top // (4 * n)
    cap = -(-capacity // 16) * 16
    rows = n * cap
    late = rows // GROUPS
    tiles = hid // min(256, part)
    scaled = (gate_prob[:, :, None] * hidden.astype(F32)).astype(BF16)
    scaled = scaled.transpose(1, 0, 2).reshape(top * tokens, part)
    vmem = pl.BlockSpec(memory_space=pltpu.VMEM)
    dma = pltpu.SemaphoreType.DMA
    grads, poly, scale, picked = pl.pallas_call(
        functools.partial(kernel, n, ndp, cap),
        out_shape=[
            jax.ShapeDtypeStruct((hid, width), BF16),
            jax.ShapeDtypeStruct((hid, hid), BF16),
            jax.ShapeDtypeStruct((8, 128), F32),
            jax.ShapeDtypeStruct((top, tokens, part), BF16),
        ],
        in_specs=[vmem] * 5,
        out_specs=[vmem] * 4,
        scratch_shapes=[
            pltpu.VMEM((n, tokens), F32),
            pltpu.VMEM((n, tokens), F32),
            pltpu.VMEM((rows, top * tokens), BF16),
            pltpu.VMEM((rows, width), BF16),
            pltpu.VMEM((rows, width), BF16),
            pltpu.VMEM((rows, part), BF16),
            pltpu.VMEM((ndp, rows, part), BF16),
            pltpu.VMEM((hid, rows - late), BF16),
            pltpu.VMEM((hid, late), BF16),
            pltpu.VMEM((ndp, rows, part), BF16),
            pltpu.VMEM((ndp - 1, rows, part), BF16),
            pltpu.VMEM((rows, part), BF16),
            pltpu.VMEM((rows, part), BF16),
            pltpu.VMEM((hid, hid), BF16),
            pltpu.VMEM((ndp - 1, hid, hid), BF16),
            pltpu.VMEM((late, hid), BF16),
            pltpu.VMEM((ndp - 1, late, hid), BF16),
            pltpu.VMEM((hid, hid), F32),
            pltpu.VMEM((hid, hid), BF16),
        ] + [dma((n,))] * 6 + [dma((ndp, GROUPS))] * 4 + [dma((ndp, tiles))] * 2 + [dma((ndp,))] * 2,
        compiler_params=pltpu.CompilerParams(
            collective_id=0, has_side_effects=True, vmem_limit_bytes=62 * 1024 * 1024
        ),
        cost_estimate=pl.CostEstimate(flops=20_000_000_000, bytes_accessed=16_000_000, transcendentals=0),
    )(expert_ids.T, gate_prob, grad_out, scaled, weights[0])
    chunk = min(256, width)
    update = pl.pallas_call(
        update_kernel,
        grid=(width // chunk,),
        out_shape=jax.ShapeDtypeStruct((hid, width), F32),
        in_specs=[
            pl.BlockSpec((8, 128), lambda c: (0, 0)),
            pl.BlockSpec((hid, hid), lambda c: (0, 0)),
            pl.BlockSpec((hid, chunk), lambda c: (0, c)),
        ],
        out_specs=pl.BlockSpec((hid, chunk), lambda c: (0, c)),
        compiler_params=pltpu.CompilerParams(vmem_limit_bytes=24 * 1024 * 1024),
        cost_estimate=pl.CostEstimate(
            flops=2 * hid * hid * width, bytes_accessed=6 * hid * width, transcendentals=0),
    )(scale, poly, grads)
    hidden_grad = picked.transpose(1, 0, 2)
    return (hidden_grad, update[None])


def solution(mesh):
    in_specs = (
        P("expert", "dp"),
        P("expert", None, "dp"),
        P("expert", None),
        P("expert", None),
        P("expert", None, "dp"),
    )
    out_specs = (P("expert", None, "dp"), P("expert", None, "dp"))
    return jax.shard_map(
        functools.partial(per_device, mesh.shape["expert"], mesh.shape["dp"]),
        mesh=mesh, in_specs=in_specs, out_specs=out_specs, check_vma=False,
    )
```

```python
import functools

import jax
import jax.numpy as jnp
from jax import lax
from jax.experimental import pallas as pl
from jax.experimental.pallas import tpu as pltpu
from jax.sharding import PartitionSpec as P

D = 4096
MESH = pl.DeviceIdType.MESH
BF16 = jnp.bfloat16
F32 = jnp.float32
GROUPS = 4


def dot(a, b, dims=((1,), (0,))):
    return lax.dot_general(a, b, (dims, ((), ())), preferred_element_type=F32)


def kernel(
    n, ndp, cap,
    ids_ref, prob_ref, grad_ref, scaled_ref, weight_ref,
    g_ref, p_ref, c_ref, picked_ref,
    rank0, rank1, select, send_grad, got_grad, send_scaled, got_scaled, scaled_t,
    back_part, back_got, summed, returned,
    gram_part, gram_got, gram_sum, a_ref,
    grad_s, grad_r, sc_s, sc_r, ret_s, ret_r, ysc_s, ysc_r, yb_s, yb_r, gram_s, gram_r,
):
    d, e = lax.axis_index("dp"), lax.axis_index("expert")
    tokens, width = grad_ref.shape
    rows = n * cap
    part = scaled_ref.shape[1]
    hid = part * ndp
    tile = min(256, part)
    tiles, per_part = hid // tile, part // tile
    own = 0
    members = n // GROUPS
    group_rows = members * cap
    chunk = min(512, width)

    def block(j):
        return pl.ds(pl.multiple_of(j * cap, 16), cap)

    def offset(j):
        return (lax.rem(j + n // 2 - 2, n - 1) + 1) * lax.div(j + n - 1, n)

    def ahead(j):
        return lax.rem(e + offset(j), n)

    def behind(j):
        return lax.rem(e + n - offset(j), n)

    def loop(lo, hi, body):
        def step(i, carry):
            body(i)
            return carry
        lax.fori_loop(lo, hi, step, 0)

    def others(body):
        loop(1, n, body)

    def dp_peer(p):
        return lax.rem(d + p, ndp)

    barrier = pltpu.get_barrier_semaphore()

    def greet(j):
        pl.semaphore_signal(barrier, inc=1, device_id=(d, ahead(j)), device_id_type=MESH)

    others(greet)
    for p in range(1, ndp):
        pl.semaphore_signal(barrier, inc=1, device_id=(dp_peer(p), e), device_id_type=MESH)

    expert_row = lax.broadcasted_iota(jnp.int32, (n, tokens), 0)
    is0 = ids_ref[0:1, :] == expert_row
    is1 = ids_ref[1:2, :] == expert_row
    named = (jnp.where(is0, 1.0, 0.0) + jnp.where(is1, 1.0, 0.0)).astype(BF16)
    earlier = lax.broadcasted_iota(jnp.int32, (tokens, tokens), 0) < lax.broadcasted_iota(
        jnp.int32, (tokens, tokens), 1
    )
    rank = dot(named, jnp.where(earlier, 1.0, 0.0).astype(BF16))
    rank0[...] = jnp.where(is0, rank, -1.0)
    rank1[...] = jnp.where(is1, rank, -1.0)

    def build(j):
        to = ahead(j)
        slot = lax.broadcasted_iota(jnp.int32, (cap, tokens), 0).astype(F32)
        for k, ref in ((0, rank0), (1, rank1)):
            select[block(j), k * tokens:(k + 1) * tokens] = jnp.where(
                ref[pl.ds(to, 1), :] == slot, 1.0, 0.0
            ).astype(BF16)

    loop(0, n, build)
    pl.semaphore_wait(barrier, n - 1 + ndp - 1)

    def scaled_copy(j, peer):
        return pltpu.make_async_remote_copy(
            src_ref=send_scaled.at[block(j)], dst_ref=got_scaled.at[d, block(j)],
            send_sem=sc_s.at[j], recv_sem=sc_r.at[j], device_id=(d, peer), device_id_type=MESH)

    def grad_copy(j, peer):
        return pltpu.make_async_remote_copy(
            src_ref=send_grad.at[block(j)], dst_ref=got_grad.at[block(j)],
            send_sem=grad_s.at[j], recv_sem=grad_r.at[j], device_id=(d, peer), device_id_type=MESH)

    def return_copy(j, peer):
        return pltpu.make_async_remote_copy(
            src_ref=summed.at[block(j)], dst_ref=returned.at[block(j)],
            send_sem=ret_s.at[j], recv_sem=ret_r.at[j], device_id=(d, peer), device_id_type=MESH)

    def across_scaled(g, p):
        at = pl.ds(g * group_rows, group_rows)
        return pltpu.make_async_remote_copy(
            src_ref=got_scaled.at[d, at], dst_ref=got_scaled.at[d, at],
            send_sem=ysc_s.at[p, g], recv_sem=ysc_r.at[p, g],
            device_id=(dp_peer(p), e), device_id_type=MESH)

    def arrived_scaled(g, p):
        at = pl.ds(g * group_rows, group_rows)
        source = lax.rem(d + ndp - p, ndp)
        return pltpu.make_async_remote_copy(
            src_ref=got_scaled.at[source, at], dst_ref=got_scaled.at[source, at],
            send_sem=ysc_s.at[p, g], recv_sem=ysc_r.at[p, g],
            device_id=(dp_peer(p), e), device_id_type=MESH)

    def across_back(g, p):
        at = pl.ds(g * group_rows, group_rows)
        return pltpu.make_async_remote_copy(
            src_ref=back_part.at[dp_peer(p), at], dst_ref=back_got.at[p - 1, at],
            send_sem=yb_s.at[p, g], recv_sem=yb_r.at[p, g],
            device_id=(dp_peer(p), e), device_id_type=MESH)

    def across_gram(i, p):
        at = (pl.ds(i * tile, tile), pl.ds(0, (i + 1) * tile))
        return pltpu.make_async_remote_copy(
            src_ref=gram_part.at[at], dst_ref=gram_got.at[(p - 1,) + at],
            send_sem=gram_s.at[p, i], recv_sem=gram_r.at[p, i],
            device_id=(dp_peer(p), e), device_id_type=MESH)

    def scaled_rows(j):
        return dot(select[block(j), :], scaled_ref[...]).astype(BF16)

    def grad_rows(j):
        chosen = select[block(j), 0:tokens] + select[block(j), tokens:2 * tokens]
        return dot(chosen, grad_ref[...]).astype(BF16)

    def put_scaled(j):
        send_scaled[block(j), :] = scaled_rows(j)
        scaled_copy(j, ahead(j)).start()

    def put_grad(j):
        send_grad[block(j), :] = grad_rows(j)
        grad_copy(j, ahead(j)).start()

    def members_of(g, body):
        first = g * members
        loop(first + (1 if first == own else 0), first + members, body)

    others(put_scaled)
    window = members * 3 // 2
    first_stop = window + members
    stops = (first_stop, first_stop + members, n)

    def put_later(j):
        send_grad[block(j), :] = grad_rows(j)
        grad_copy(j - window, ahead(j - window)).wait_send()
        grad_copy(j, ahead(j)).start()

    loop(1, window + 1, put_grad)
    got_scaled[d, 0:cap, :] = scaled_rows(own)
    got_grad[0:cap, :] = grad_rows(own)
    others(lambda j: scaled_copy(j, ahead(j)).wait_recv())
    for g in range(GROUPS):
        for p in range(1, ndp):
            across_scaled(g, p).start()

    def back_of(g):
        at = slice(g * group_rows, (g + 1) * group_rows)

        def column(i):
            term = dot(got_grad[at, :], weight_ref[pl.ds(pl.multiple_of(i * tile, tile), tile), :],
                       ((1,), (1,))).astype(BF16)
            cols = pl.ds(pl.multiple_of(lax.rem(i, per_part) * tile, tile), tile)
            back_part[lax.div(i, per_part), at, cols] = term

        loop(0, tiles, column)
        for p in range(1, ndp):
            across_back(g, p).start()

    for g in range(GROUPS - 1):
        loop(window + 1 if g == 0 else stops[g - 1], stops[g], put_later)
        members_of(g, lambda j: grad_copy(j, ahead(j)).wait_recv())
        back_of(g)
        if g == GROUPS - 3:
            for h in range(GROUPS):
                for p in range(1, ndp):
                    arrived_scaled(h, p).wait_recv()
            for b in range(ndp):
                scaled_t[b * part:(b + 1) * part, :] = got_scaled[b].T

    def give_back(g):
        at = slice(g * group_rows, (g + 1) * group_rows)
        for p in range(1, ndp):
            across_back(g, p).wait_recv()
        total = back_part[d, at, :].astype(F32)
        for p in range(1, ndp):
            total = total + back_got[p - 1, at, :].astype(F32)
        summed[at, :] = total.astype(BF16)
        members_of(g, lambda j: return_copy(j, behind(j)).start())

    members_of(GROUPS - 1, lambda j: grad_copy(j, ahead(j)).wait_recv())

    for g in range(GROUPS - 1):
        give_back(g)
    back_of(GROUPS - 1)

    for i in range(tiles):
        at = slice(i * tile, (i + 1) * tile)

        def gradient(c):
            cols = pl.ds(pl.multiple_of(c * chunk, chunk), chunk)
            g_ref[at, cols] = dot(scaled_t[at, :], got_grad[:, cols]).astype(BF16)

        def gram(j):
            other = pl.ds(pl.multiple_of(j * tile, tile), tile)
            gram_part[at, other] = dot(g_ref[at, :], g_ref[other, :], ((1,), (1,))).astype(BF16)

        loop(0, width // chunk, gradient)
        loop(0, i + 1, gram)
        for p in range(1, ndp):
            across_gram(i, p).start()
    give_back(GROUPS - 1)
    returned[own * cap:(own + 1) * cap, :] = summed[own * cap:(own + 1) * cap, :]

    squares = jnp.zeros((1, 1), F32)
    for i in range(tiles):
        at = slice(i * tile, (i + 1) * tile)
        for p in range(1, ndp):
            across_gram(i, p).wait_recv()
        for j in range(i + 1):
            other = slice(j * tile, (j + 1) * tile)
            total = gram_part[at, other].astype(F32)
            for p in range(1, ndp):
                total = total + gram_got[p - 1, at, other].astype(F32)
            gram_sum[at, other] = total
            here = jnp.sum(jnp.sum(total * total, axis=0, keepdims=True), axis=1, keepdims=True)
            squares = squares + here * (1.0 if i == j else 2.0)
    norm_sq = jnp.sqrt(squares) + 1e-6
    inverse = 1.0 / norm_sq
    scale = lax.rsqrt(norm_sq) * (D**0.5)
    c_ref[...] = jnp.broadcast_to(2.25 * scale, c_ref.shape)
    for i in range(tiles):
        at = slice(i * tile, (i + 1) * tile)
        for j in range(i + 1):
            other = slice(j * tile, (j + 1) * tile)
            value = gram_sum[at, other] * inverse
            a_ref[at, other] = value.astype(BF16)
            if j < i:
                a_ref[other, at] = value.T.astype(BF16)

    for p in range(1, ndp):
        for i in range(tiles):
            across_gram(i, p).wait_send()
    a2_ref, w_ref = gram_part, gram_got.at[0]

    def square(i):
        at = pl.ds(pl.multiple_of(i * tile, tile), tile)
        a2 = dot(a_ref[at, :], a_ref[...])
        a1 = a_ref[at, :].astype(F32)
        a2_ref[at, :] = a2.astype(BF16)
        w_ref[at, :] = (1.125 * a1 - 0.125 * a2).astype(BF16)
        gram_sum[at, :] = 1.6875 * a2 - 2.4375 * a1

    def finish(i):
        at = pl.ds(pl.multiple_of(i * tile, tile), tile)
        last = dot(a2_ref[at, :], w_ref[...])
        p_ref[at, :] = ((gram_sum[at, :] - 0.5 * last) * scale).astype(BF16)

    loop(0, tiles, square)
    loop(0, tiles, finish)

    others(lambda j: return_copy(j, behind(j)).wait_recv())
    step = min(256, tokens)
    for k in range(2):
        for t in range(0, tokens, step):
            cols = slice(k * tokens + t, k * tokens + t + step)
            value = dot(select[:, cols], returned[...], ((0,), (0,)))
            picked_ref[k, t:t + step, :] = (prob_ref[t:t + step, k:k + 1] * value).astype(BF16)

    def drain(j):
        scaled_copy(j, ahead(j)).wait_send()
        return_copy(j, behind(j)).wait_send()

    others(drain)
    loop(n - window, n, lambda j: grad_copy(j, ahead(j)).wait_send())
    for p in range(1, ndp):
        for g in range(GROUPS):
            across_scaled(g, p).wait_send()
            across_back(g, p).wait_send()


def update_kernel(c_ref, p_ref, g_ref, out_ref):
    grads = g_ref[...]
    out_ref[...] = dot(p_ref[...], grads) + grads.astype(F32) * c_ref[0:1, 0:1]


def per_device(n, ndp, grad_out, hidden, gate_prob, expert_ids, weights):
    tokens, width = grad_out.shape
    top = expert_ids.shape[1]
    part = hidden.shape[2]
    hid = part * ndp
    capacity = 5 * tokens * top // (4 * n)
    cap = -(-capacity // 16) * 16
    rows = n * cap
    tiles = hid // min(256, part)
    scaled = (gate_prob[:, :, None] * hidden.astype(F32)).astype(BF16)
    scaled = scaled.transpose(1, 0, 2).reshape(top * tokens, part)
    vmem = pl.BlockSpec(memory_space=pltpu.VMEM)
    dma = pltpu.SemaphoreType.DMA
    grads, poly, scale, picked = pl.pallas_call(
        functools.partial(kernel, n, ndp, cap),
        out_shape=[
            jax.ShapeDtypeStruct((hid, width), BF16),
            jax.ShapeDtypeStruct((hid, hid), BF16),
            jax.ShapeDtypeStruct((8, 128), F32),
            jax.ShapeDtypeStruct((top, tokens, part), BF16),
        ],
        in_specs=[vmem] * 5,
        out_specs=[vmem] * 4,
        scratch_shapes=[
            pltpu.VMEM((n, tokens), F32),
            pltpu.VMEM((n, tokens), F32),
            pltpu.VMEM((rows, top * tokens), BF16),
            pltpu.VMEM((rows, width), BF16),
            pltpu.VMEM((rows, width), BF16),
            pltpu.VMEM((rows, part), BF16),
            pltpu.VMEM((ndp, rows, part), BF16),
            pltpu.VMEM((hid, rows), BF16),
            pltpu.VMEM((ndp, rows, part), BF16),
            pltpu.VMEM((ndp - 1, rows, part), BF16),
            pltpu.VMEM((rows, part), BF16),
            pltpu.VMEM((rows, part), BF16),
            pltpu.VMEM((hid, hid), BF16),
            pltpu.VMEM((ndp - 1, hid, hid), BF16),
            pltpu.VMEM((hid, hid), F32),
            pltpu.VMEM((hid, hid), BF16),
        ] + [dma((n,))] * 6 + [dma((ndp, GROUPS))] * 4 + [dma((ndp, tiles))] * 2,
        compiler_params=pltpu.CompilerParams(
            collective_id=0, has_side_effects=True, vmem_limit_bytes=62 * 1024 * 1024
        ),
        cost_estimate=pl.CostEstimate(flops=20_000_000_000, bytes_accessed=16_000_000, transcendentals=0),
    )(expert_ids.T, gate_prob, grad_out, scaled, weights[0])
    chunk = min(256, width)
    update = pl.pallas_call(
        update_kernel,
        grid=(width // chunk,),
        out_shape=jax.ShapeDtypeStruct((hid, width), F32),
        in_specs=[
            pl.BlockSpec((8, 128), lambda c: (0, 0)),
            pl.BlockSpec((hid, hid), lambda c: (0, 0)),
            pl.BlockSpec((hid, chunk), lambda c: (0, c)),
        ],
        out_specs=pl.BlockSpec((hid, chunk), lambda c: (0, c)),
        compiler_params=pltpu.CompilerParams(vmem_limit_bytes=24 * 1024 * 1024),
        cost_estimate=pl.CostEstimate(
            flops=2 * hid * hid * width, bytes_accessed=6 * hid * width, transcendentals=0),
    )(scale, poly, grads)
    hidden_grad = picked.transpose(1, 0, 2)
    return (hidden_grad, update[None])


def solution(mesh):
    in_specs = (
        P("expert", "dp"),
        P("expert", None, "dp"),
        P("expert", None),
        P("expert", None),
        P("expert", None, "dp"),
    )
    out_specs = (P("expert", None, "dp"), P("expert", None, "dp"))
    return jax.shard_map(
        functools.partial(per_device, mesh.shape["expert"], mesh.shape["dp"]),
        mesh=mesh, in_specs=in_specs, out_specs=out_specs, check_vma=False,
    )
```
